128 devices in a mesh: dp: 64 (over z, y, x_hi, core), seq: 2 (over x_lo).
Axes of the slice: x: 4 (x_hi: 2, x_lo: 2; x = x_hi * 2 + x_lo), y: 4, z: 4, core: 2. Of those that a mesh axis runs over, the one named last changes fastest.
Arguments:
- inputs: bfloat16 [128, 512, 768], P('dp', 'seq'), may hold values from -6 to 6
- memory: bfloat16 [128, 256, 768], P('dp', 'seq'), may hold values from -6 to 6
- cotangent: bfloat16 [128, 512, 768], P('dp', 'seq'), may hold values from -6 to 6
- seg_ids: int32 [128, 512], P('dp', 'seq'), may hold values from 0 to 7, as said below
- mem_seg: int32 [128, 256], P('dp', 'seq'), may hold values from 0 to 7, as said below
- tasks: int32 [128], P('dp'), may hold values from 0 to 7
- self_qkv: bfloat16 [768, 2304], P('dp'), may hold values from -0.21875 to 0.21875
- self_out: bfloat16 [768, 768], P('dp'), may hold values from -1.25 to 1.25
- cross_query: bfloat16 [768, 768], P('dp'), may hold values from -0.21875 to 0.21875
- cross_kv: bfloat16 [768, 1536], P('dp'), may hold values from -0.21875 to 0.21875
- cross_out: bfloat16 [768, 768], P('dp'), may hold values from -1.25 to 1.25
- ff_in: bfloat16 [768, 3072], P('dp'), may hold values from -0.21875 to 0.21875
- ff_out: bfloat16 [3072, 768], P('dp'), may hold values from -0.109375 to 0.109375
- gen_down: bfloat16 [64, 18432], P(None, 'dp'), may hold values from -0.0390625 to 0.0390625
- gen_up: bfloat16 [64, 18432], P(None, 'dp'), may hold values from -0.21875 to 0.21875
- gen_gain: bfloat16 [64, 768], P(None, 'dp'), may hold values from -0.375 to 0.375
- task_table: float32 [8, 64], replicated, may hold values from -6 to 6
- place_table: float32 [3, 64], replicated, may hold values from -6 to 6
- proj_in: float32 [128, 128], replicated, may hold values from -0.5 to 0.5
- proj_out: float32 [128, 64], replicated, may hold values from -0.5 to 0.5
Outputs:
- mixed: bfloat16 [128, 512, 768], P('dp', 'seq')
- grad_input: float32 [128, 512, 768], P('dp', 'seq')
- grad_memory: float32 [128, 256, 768], P('dp', 'seq')
- grad_self_qkv: float32 [768, 2304], P('dp')
- grad_self_out: float32 [768, 768], P('dp')
- grad_cross_query: float32 [768, 768], P('dp')
- grad_cross_kv: float32 [768, 1536], P('dp')
- grad_cross_out: float32 [768, 768], P('dp')
- grad_ff_in: float32 [768, 3072], P('dp')
- grad_ff_out: float32 [3072, 768], P('dp')
- grad_gen_down: float32 [64, 18432], P(None, 'dp')
- grad_gen_up: float32 [64, 18432], P(None, 'dp')
- grad_gen_gain: float32 [64, 768], P(None, 'dp')
- task_embedding_gradient: float32 [8, 64], replicated
- grad_place_table: float32 [3, 64], replicated
- grad_proj_in: float32 [128, 128], replicated
- output_projection_gradient: float32 [128, 64], replicated
The draws below stay inside these ranges and needn't reach their ends.
Inputs may be any that keep to these rules, and one draw needn't show every extreme that they name: `seg_ids`: within each pack the ids never fall from row to row and every id occurs. `mem_seg`: within each pack the ids never fall from row to row and every id occurs.
All inputs are finite; a program needn't handle non-finite values.
Results may differ from the reference program's by a relative error of at most 0.03.
The reference program's roundings to bfloat16 on the way count: a program that leaves them out, or rounds other values in their place, can miss the bound.
Values may be sent and summed in bfloat16 or wider, within the bound.
No kernel may reach another device: no remote copies, remote signals or barrier semaphores. Data moves between devices by JAX's collectives and lax.ppermute only.
A program may use at most 256 MiB of HBM per device.

```python
import math
import jax
import jax.numpy as jnp
from jax import lax

D = 768
HEADS = 12
HD = 64
FF = 3072
R = 24
TE = 64
HH = 128
NTASK = 8
PACK = 512
MEM = 256
NSEG = 8
TOTAL_PACKS = 128
N_SEQ = 2


def document_ids(key, length, doc_count):
    margin = length // 8
    middle = length // 2
    places = jnp.arange(1, length, dtype=jnp.int32)
    allowed = (places <= middle - margin) | (places > middle + margin)
    random_part = jax.random.randint(key, (length - 1,), 0, 1 << 20, dtype=jnp.int32)
    scores = jnp.where(allowed, random_part * length + places, -1)
    chosen = lax.top_k(scores, doc_count - 1)[0] % length
    row_ids = jnp.arange(length, dtype=jnp.int32)
    return jnp.sum((row_ids[:, None] >= chosen[None, :]).astype(jnp.int32), axis=1)


def draw_seg_ids(key, part):
    key = jax.random.fold_in(key, 11)
    pack_keys = jax.random.split(key, TOTAL_PACKS)
    return jax.vmap(lambda single_key: document_ids(single_key, PACK, NSEG))(pack_keys)


def draw_mem_seg(key, part):
    key = jax.random.fold_in(key, 23)
    pack_keys = jax.random.split(key, TOTAL_PACKS)
    return jax.vmap(lambda single_key: document_ids(single_key, MEM, NSEG))(pack_keys)


def place_ends(values, own_key, least, top_value):
    longest = values.shape.index(max(values.shape))
    spots = []
    for shift in (0, 1):
        where = [jax.random.randint(jax.random.fold_in(own_key, axis), (), 0, length) for axis, length in enumerate(values.shape)]
        where[longest] = (where[longest] + shift) % values.shape[longest]
        spots.append(tuple(where))
    return values.at[spots[0]].set(least).at[spots[1]].set(top_value)


def steps_of(key, extent, cuts, least, top_value):
    def one(dim, parts):
        draws = jax.random.uniform(jax.random.fold_in(jax.random.fold_in(key, 6), dim), (parts,), jnp.float32, least / len(cuts), top_value / len(cuts))
        return jnp.repeat(jnp.exp(draws), extent[dim] // parts).reshape((-1,) + (1,) * (len(extent) - dim - 1))

    loudness = one(*cuts[0])
    for cut in cuts[1:]:
        loudness = loudness * one(*cut)
    return loudness


def scatter_about(own_key, dims, spread, limit, cuts=(), kind=jnp.bfloat16):
    factor_of = steps_of(own_key, dims, cuts, -0.22, 0.18) if cuts else 1.0
    drawn = jax.random.normal(own_key, dims, jnp.float32) * spread * factor_of
    return jnp.minimum(jnp.maximum(drawn, -limit), limit).astype(kind)


def setup_inputs(seed: int = 0) -> dict:
    key_of = jax.random.split(jax.random.key(seed), 21)
    return {
        "inputs": scatter_about(key_of[0], (TOTAL_PACKS, PACK, D), 1.0, 6.0, ((0, 64), (1, 2))),
        "memory": scatter_about(key_of[1], (TOTAL_PACKS, MEM, D), 1.0, 6.0, ((0, 64), (1, 2))),
        "cotangent": scatter_about(key_of[2], (TOTAL_PACKS, PACK, D), 1.0, 6.0, ((0, 64), (1, 2))),
        "seg_ids": draw_seg_ids(jax.random.fold_in(key_of[20], 71), 0),
        "mem_seg": draw_mem_seg(jax.random.fold_in(key_of[20], 71), 0),
        "tasks": place_ends(jax.random.randint(key_of[5], (TOTAL_PACKS,), 0, NTASK), jax.random.fold_in(key_of[5], 1), 0, NTASK - 1).astype(jnp.int32),
        "self_qkv": scatter_about(key_of[6], (D, 3 * D), D ** -0.5, 0.21875, ((0, 64),)),
        "self_out": scatter_about(key_of[7], (D, D), (D // 32) ** -0.5, 1.25, ((0, 64),)),
        "cross_query": scatter_about(key_of[8], (D, D), D ** -0.5, 0.21875, ((0, 64),)),
        "cross_kv": scatter_about(key_of[9], (D, 2 * D), D ** -0.5, 0.21875, ((0, 64),)),
        "cross_out": scatter_about(key_of[10], (D, D), (D // 32) ** -0.5, 1.25, ((0, 64),)),
        "ff_in": scatter_about(key_of[11], (D, FF), D ** -0.5, 0.21875, ((0, 64),)),
        "ff_out": scatter_about(key_of[12], (FF, D), FF ** -0.5, 0.109375, ((0, 64),)),
        "gen_down": scatter_about(key_of[13], (TE, D * R), (TE * D // 2) ** -0.5, 0.0390625, ((1, 64),)),
        "gen_up": scatter_about(key_of[14], (TE, R * D), (TE * R // 2) ** -0.5, 0.21875, ((1, 64),)),
        "gen_gain": scatter_about(key_of[15], (TE, D), (TE * 4) ** -0.5, 0.375, ((1, 64),)),
        "task_table": scatter_about(key_of[16], (NTASK, TE), 1.0, 6.0, (), jnp.float32),
        "place_table": scatter_about(key_of[17], (3, TE), 1.0, 6.0, (), jnp.float32),
        "proj_in": scatter_about(key_of[18], (2 * TE, HH), (2 * TE) ** -0.5, 0.5, (), jnp.float32),
        "proj_out": scatter_about(key_of[19], (HH, TE), HH ** -0.5, 0.5, (), jnp.float32),
    }


@jax.custom_vjp
def low(v):
    return lax.optimization_barrier(v.astype(jnp.bfloat16)).astype(jnp.float32)

@jax.custom_vjp
def reduced_precision_backward(v):
    return v

def low_keep(v):
    return (low(v), None)

def low_pass(kept, grad):
    return (grad,)

def back_keep(v):
    return (v, None)

def back_low(kept, grad):
    return (low(grad),)
low.defvjp(low_keep, low_pass)
reduced_precision_backward.defvjp(back_keep, back_low)
epsilon = 1e-06
masked_out = -1e+30
highest_precision = lax.Precision.HIGHEST

def round_both(value):
    return low(reduced_precision_backward(value))

def matmul(left, right):
    return jnp.dot(left, right, precision=highest_precision)

def rms_norm(resid, gains):
    inverse = lax.rsqrt(lax.optimization_barrier(jnp.mean(resid * resid, axis=-1, keepdims=True)) + epsilon)
    return resid * inverse * gains

def attend(queries, keys, values, mask):
    score_scale = 1.0 / math.sqrt(HD)
    query_heads = queries.reshape(queries.shape[0], HEADS, HD)
    key_heads = keys.reshape(keys.shape[0], HEADS, HD)
    value_heads = values.reshape(values.shape[0], HEADS, HD)
    scores = reduced_precision_backward(jnp.einsum('qhd,khd->hqk', query_heads, key_heads, precision=highest_precision) * score_scale)
    scores = jnp.where(mask[None], scores, masked_out)
    softmax_prob = jax.nn.softmax(scores, axis=-1)
    attn_out = jnp.einsum('hqk,khd->qhd', low(softmax_prob), value_heads, precision=highest_precision)
    return round_both(attn_out.reshape(queries.shape[0], D))

def adapter(branch, down_blocks, up_projection_blocks):
    blocks = down_blocks.shape[0]
    branch_low = low(branch).reshape(blocks, -1, D)
    pre_act = reduced_precision_backward(jnp.einsum('brd,bdk->brk', branch_low, down_blocks, precision=highest_precision))
    hidden_state = low(jax.nn.gelu(pre_act))
    layer_result = reduced_precision_backward(jnp.einsum('oem,oml->oel', hidden_state, up_projection_blocks, precision=highest_precision))
    return layer_result.reshape(-1, D)

def hyper_code(onehot, task_table, place_table, proj_in, proj_out):
    embedding = matmul(onehot, task_table)
    places = place_table.shape[0]
    joined_in = jnp.concatenate([jnp.broadcast_to(embedding[None, :], (places, TE)), place_table], axis=1)
    return matmul(jax.nn.gelu(matmul(joined_in, proj_in)), proj_out)

def pack_layer(params, row_in, mem_in, doc_ids, mem_docs, task_id):
    self_qkv, self_out, cross_query, cross_kv, cross_out, ff_in, ff_out, gen_down, gen_up, gen_gain, task_table, place_table, proj_in, proj_out = params
    onehot = (jnp.arange(NTASK, dtype=jnp.int32) == task_id).astype(jnp.float32)
    code_low = low(hyper_code(onehot, task_table, place_table, proj_in, proj_out))
    down_gen = low(matmul(code_low, gen_down)).reshape(3, D, R)
    up_gen = low(matmul(code_low, gen_up)).reshape(3, R, D)
    norm_gains = 1.0 + matmul(code_low, gen_gain)
    down_blocks = reduced_precision_backward(jnp.broadcast_to(down_gen[None], (N_SEQ, 3, D, R)))
    up_projection_blocks = reduced_precision_backward(jnp.broadcast_to(up_gen[None], (N_SEQ, 3, R, D)))
    positions = jnp.arange(PACK)
    self_mask = (doc_ids[:, None] == doc_ids[None, :]) & (positions[None, :] <= positions[:, None])
    cross_mask = doc_ids[:, None] == mem_docs[None, :]
    normed = low(rms_norm(row_in, norm_gains[0]))
    self_proj = round_both(matmul(normed, self_qkv))
    attended = attend(self_proj[:, :D], self_proj[:, D:2 * D], self_proj[:, 2 * D:], self_mask)
    branch = reduced_precision_backward(matmul(attended, self_out))
    after_self = row_in + branch + adapter(branch, down_blocks[:, 0], up_projection_blocks[:, 0])
    normed = low(rms_norm(after_self, norm_gains[1]))
    queries = round_both(matmul(normed, cross_query))
    keys_vals = round_both(matmul(mem_in, cross_kv))
    attended = attend(queries, keys_vals[:, :D], keys_vals[:, D:], cross_mask)
    branch = reduced_precision_backward(matmul(attended, cross_out))
    second = after_self + branch + adapter(branch, down_blocks[:, 1], up_projection_blocks[:, 1])
    normed = low(rms_norm(second, norm_gains[2]))
    ff_hidden = reduced_precision_backward(matmul(normed, ff_in))
    branch = reduced_precision_backward(matmul(low(jax.nn.gelu(ff_hidden)), ff_out))
    return second + branch + adapter(branch, down_blocks[:, 2], up_projection_blocks[:, 2])

def reference(inputs, memory, cotangent, seg_ids, mem_seg, tasks, self_qkv, self_out, cross_query, cross_kv, cross_out, ff_in, ff_out, gen_down, gen_up, gen_gain, task_table, place_table, proj_in, proj_out):
    params = (self_qkv.astype(jnp.float32), self_out.astype(jnp.float32), cross_query.astype(jnp.float32), cross_kv.astype(jnp.float32), cross_out.astype(jnp.float32), ff_in.astype(jnp.float32), ff_out.astype(jnp.float32), gen_down.astype(jnp.float32), gen_up.astype(jnp.float32), gen_gain.astype(jnp.float32), task_table, place_table, proj_in, proj_out)
    layer_saved = jax.checkpoint(pack_layer)

    def forward(rows_all, mem_all, weights):

        def scan_step(carried, pack_item):
            return (carried, layer_saved(weights, *pack_item))
        _, layer_result = lax.scan(scan_step, jnp.zeros((), jnp.float32), (rows_all, mem_all, seg_ids, mem_seg, tasks))
        return layer_result
    layer_result, pull_back = jax.vjp(forward, inputs.astype(jnp.float32), memory.astype(jnp.float32), params)
    grad_rows, grad_mem, gradients = pull_back(cotangent.astype(jnp.float32))
    return (layer_result.astype(jnp.bfloat16), grad_rows, grad_mem, gradients[0], gradients[1], gradients[2], gradients[3], gradients[4], gradients[5], gradients[6], gradients[7], gradients[8], gradients[9], gradients[10], gradients[11], gradients[12], gradients[13])
```

```python
from functools import partial
import math

import jax
import jax.numpy as jnp
from jax import lax
from jax.experimental import pallas as pl
from jax.experimental.pallas import tpu as pltpu
from jax.sharding import PartitionSpec as P

D = 768
HEADS = 12
HD = 64
PAIRS = HEADS // 2
FF = 3072
R = 24
NTASK = 8
TE = 64
WIDE = NTASK * R
PLACE = 256
ROWS = 256

epsilon = 1e-06
masked_out = -1e30
highest_precision = lax.Precision.HIGHEST
low = jnp.bfloat16
full = jnp.float32
scale = 1.0 / math.sqrt(HD)


def mm(left, right):
    return jnp.dot(left, right, preferred_element_type=full)


def swap(value, axis, mask):
    count = lax.axis_size(axis)
    return lax.ppermute(value, axis, [(i, i ^ mask) for i in range(count)])


def group_exchange(value):
    me = lax.axis_index("dp") % 4
    got = [lax.dynamic_index_in_dim(value, me, 0, keepdims=False)]
    for step in (1, 2, 3):
        got.append(swap(lax.dynamic_index_in_dim(value, me ^ step, 0, keepdims=False), "dp", step))
    got = jnp.stack(got)
    return jnp.take(got, jnp.arange(4) ^ me, axis=0)


def from_quarters(rows48):
    cols = rows48.shape[1]
    pieces = group_exchange(rows48.reshape(4, 12, cols))
    return pieces.transpose(1, 0, 2).reshape(12, 4 * cols)


WEIGHTS = (
    ("self_out", 0, 768),
    ("query", 768, 768),
    ("cross_out", 1536, 768),
    ("mem_kv", 2304, 1536),
    ("down", 3840, 512),
    ("ff_in", 4608, 3072),
)
QUARTER = 1920
FF_ROWS = 128
EARLY = 640


def early_gather(block):
    along_x = jnp.stack([block, swap(block, "dp", 2)])
    along_z = jnp.stack([along_x] + [swap(along_x, "dp", step << 4) for step in (1, 2, 3)])
    return jnp.stack([along_z] + [swap(along_z, "dp", step << 2) for step in (1, 2, 3)])


def unpack_early(own, other):
    dp = lax.axis_index("dp")

    def body(place_ref, own_ref, other_ref, qkv, down):
        for mine in range(4):

            @pl.when(place_ref[2] == mine)
            def _():
                for q in range(4):
                    step = q ^ mine
                    src = (own_ref, other_ref)[step % 2]
                    if q < 3:
                        qkv[0, :, EARLY * q : EARLY * (q + 1)] = src[0, 0, step // 2]
                    else:
                        qkv[0, :, EARLY * q :] = src[0, 0, step // 2, :, : 2304 - 3 * EARLY]
                        down[0] = src[0, 0, step // 2, :, 2304 - 3 * EARLY :]

    def place_of(g, place):
        return ((g % 4) ^ place[1], (g // 4) ^ place[0], 0, 0, 0)

    return pl.pallas_call(
        body,
        grid_spec=pltpu.PrefetchScalarGridSpec(
            num_scalar_prefetch=1,
            grid=(16,),
            in_specs=[pl.BlockSpec((1, 1, 2, 48, EARLY), place_of)] * 2,
            out_specs=[
                pl.BlockSpec((1, 48, 2304), lambda g, place: (g, 0, 0)),
                pl.BlockSpec((1, 48, PLACE), lambda g, place: (g, 0, 0)),
            ],
        ),
        out_shape=[jax.ShapeDtypeStruct((16, 48, 2304), low), jax.ShapeDtypeStruct((16, 48, PLACE), low)],
        compiler_params=pltpu.CompilerParams(vmem_limit_bytes=6 * 2**20),
        name="unpack_early",
    )(jnp.stack([dp // 16, (dp // 4) % 4, dp % 4]).astype(jnp.int32), own, other)


def up_tiles():
    for block in (0, 1):
        for j in range(3):
            k, half = divmod(3 * block + j, 2)
            for piece in range(3):
                lane, row = divmod(3 * j + piece, 6)
                yield block, 8 * row, 128 * lane, 8 * k, 384 * half + 128 * piece


def unpack(gathered):
    def body(src, *outs):
        for (_, start, width), out in zip(WEIGHTS, outs):
            for q in range(4):
                first, last = max(start, q * QUARTER), min(start + width, (q + 1) * QUARTER)
                if first < last:
                    out[:, :, first - start : last - start] = src[
                        :, q, :, first - q * QUARTER : last - q * QUARTER
                    ]
        outs[-2][...] = src[:, :, :, 1920:2688]
        for place in range(3):
            blocks = [src[block, place, :, 2688:2944].astype(full) for block in (0, 1)]
            for block, row, lane, to_row, to_lane in up_tiles():
                outs[-1][place, to_row : to_row + 8, to_lane : to_lane + 128] = blocks[block][
                    row : row + 8, lane : lane + 128
                ]

    shapes = [(16, 48, width) for _, _, width in WEIGHTS] + [(16, 4, 48, 768)]
    return pl.pallas_call(
        body,
        grid=(8,),
        out_shape=[jax.ShapeDtypeStruct(shape, low) for shape in shapes]
        + [jax.ShapeDtypeStruct((3, WIDE, D), full)],
        in_specs=[pl.BlockSpec((2, 4, 48, 2944), lambda g: (g, 0, 0, 0))],
        out_specs=[
            pl.BlockSpec((2, *shape[1:]), (lambda g: (g, 0, 0)) if len(shape) == 3 else (lambda g: (g, 0, 0, 0)))
            for shape in shapes
        ]
        + [pl.BlockSpec((3, R, D), lambda g: (0, g, 0))],
        compiler_params=pltpu.CompilerParams(vmem_limit_bytes=16 * 2**20),
        name="unpack_weights",
    )(gathered)


def pack_ff(grad_in, grad_out):
    def body(gin, gout, out):
        for q in range(4):
            out[0, q, :48, :] = gin[0, :, 768 * q : 768 * (q + 1)]
            out[0, q, 48:96, :] = gout[0, q]
            out[0, q, 96:, :] = jnp.zeros((FF_ROWS - 96, D), low)

    return pl.pallas_call(
        body,
        grid=(16,),
        out_shape=jax.ShapeDtypeStruct((16, 4, FF_ROWS, D), low),
        in_specs=[
            pl.BlockSpec((1, 48, FF), lambda g: (g, 0, 0)),
            pl.BlockSpec((1, 4, 48, D), lambda g: (g, 0, 0, 0)),
        ],
        out_specs=pl.BlockSpec((1, 4, FF_ROWS, D), lambda g: (g, 0, 0, 0)),
        compiler_params=pltpu.CompilerParams(vmem_limit_bytes=6 * 2**20),
        name="pack_ff",
    )(grad_in.reshape(16, 48, FF), grad_out.reshape(16, 4, 48, D)).reshape(64, FF_ROWS, D)


def pack_gradients(core, lefts, jobs, downs, gain, ups, widths):
    quarter = sum(widths) - 256
    count = len(jobs)
    segments = []
    bounds = [sum(widths[:i]) for i in range(len(widths) + 1)]

    def add(source, source_lane, q, lane, width):
        for part in range(len(widths)):
            first, last = max(lane, bounds[part]), min(lane + width, bounds[part + 1])
            if first < last:
                segments.append((source, source_lane + first - lane, q, part, first - bounds[part], last - first))

    for column in range(count + 1):
        for q in range(4):
            first, last = max(column * D, q * quarter), min(column * D + D, (q + 1) * quarter)
            if first < last:
                add(column, first - column * D, q, first - q * quarter, last - first)
    for q in range(3):
        add(None, 0, q, quarter, 256)
    filled = (count + 1) * D - 3 * quarter
    add("nothing", 0, 3, filled, sum(widths) - filled)
    rows = 384

    def body(core_ref, *rest):
        left_refs, rest = rest[: len(lefts)], rest[len(lefts) :]
        right_refs, rest = rest[:count], rest[count:]
        down_refs, gain_ref, tables, outs, made = rest[:3], rest[3], rest[4:7], rest[7:-1], rest[-1]
        first_down = down_refs[0][...] + gain_ref[...]
        made[count, :, :PLACE] = first_down
        for place in (1, 2):
            made[count, :, place * PLACE : (place + 1) * PLACE] = down_refs[place][...]
        for index, left in enumerate(left_refs):
            turned = left[...].reshape(-1, rows).T
            for job, (of_left, _, _) in enumerate(jobs):
                if of_left == index:
                    right = right_refs[job][...].reshape(-1, D)
                    made[job] = mm(turned, right).astype(low)
        blocks = []
        for place in range(3):
            by_lane = {0: [], 128: []}
            for pair in range(rows // 96):
                tiles = {
                    (block, row, lane): tables[place][R * pair + from_row : R * pair + from_row + 8, from_lane : from_lane + 128]
                    for block, row, lane, from_row, from_lane in up_tiles()
                }
                nothing = jnp.zeros((8, 128), full)
                for lane in (0, 128):
                    by_lane[lane] += [
                        tiles.get((block, 8 * row, lane), nothing) for block in (0, 1) for row in range(6)
                    ]
            blocks.append([jnp.concatenate(by_lane[lane], axis=0).astype(low) for lane in (0, 128)])
        for mine in (0, 1):

            @pl.when(core_ref[0] == mine)
            def _():
                for column, from_lane, q, part, lane, width in segments:
                    out = outs[2 * part + (q % 2 != mine)]
                    lanes = slice(from_lane, from_lane + width)
                    if column is None:
                        for piece in range(width // 128):
                            out[q // 2, :, lane + 128 * piece : lane + 128 * (piece + 1)] = blocks[q][
                                from_lane // 128 + piece
                            ]
                    elif column == "nothing":
                        out[q // 2, :, lane : lane + width] = jnp.zeros((rows, width), low)
                    elif column == 5:
                        out[q // 2, :, lane : lane + width] = made[count, :, lanes]
                    else:
                        out[q // 2, :, lane : lane + width] = made[column - (column > 5), :, lanes]

    shapes = [(2, D, width) for width in widths for _ in range(2)]
    whole = pl.Buffered(1)
    outs = pl.pallas_call(
        body,
        grid=(D // rows,),
        out_shape=[jax.ShapeDtypeStruct(shape, low) for shape in shapes],
        in_specs=[pl.BlockSpec(memory_space=pltpu.SMEM)]
        + [pl.BlockSpec((2, length, rows), partial(lambda block, g: (0, block, g), block)) for _, block, length in lefts]
        + [
            pl.BlockSpec((2, length, D), partial(lambda block, g: (0, block, 0), block), pipeline_mode=whole)
            for (_, right, block), length in zip(jobs, [lefts[of_left][2] for of_left, _, _ in jobs])
        ]
        + [pl.BlockSpec((rows, PLACE), lambda g: (g, 0))] * 4
        + [pl.BlockSpec((R * rows // 96, D), lambda g: (g, 0))] * 3,
        out_specs=[pl.BlockSpec((2, rows, shape[2]), lambda g: (0, g, 0)) for shape in shapes],
        scratch_shapes=[pltpu.VMEM((count + 1, rows, D), low)],
        compiler_params=pltpu.CompilerParams(vmem_limit_bytes=32 * 2**20),
        cost_estimate=pl.CostEstimate(flops=1, bytes_accessed=1, transcendentals=0),
        name="pack_gradients",
    )(core.reshape(1), *[left for left, _, _ in lefts], *[right for _, right, _ in jobs], *downs, gain, *ups)
    return outs[0::2], outs[1::2]


def over_cores(send):
    return [swap(part, "dp", 1) for part in send]


def ring_order(part):
    dp = lax.axis_index("dp")
    y, z = (dp // 4) % 4, dp // 16
    along_y, along_z = (2, y, 2), (1, z, 4)
    return (along_y, along_z) if part % 2 == 0 else (along_z, along_y)


def first_piece(keep, got, part, step):
    axis, position, _ = ring_order(part)[0]
    shape = (2, 4, 4, 48, keep.shape[2])
    mine = lax.dynamic_index_in_dim(keep.reshape(shape), position ^ step, axis, keepdims=False)
    other = lax.dynamic_index_in_dim(got.reshape(shape), position ^ step, axis, keepdims=False)
    return mine.astype(full) + other.astype(full)


def first_exchange(keep, got):
    return [
        [
            swap(first_piece(keep[part], got[part], part, step).astype(low), "dp", step << ring_order(part)[0][2])
            for step in (1, 2, 3)
        ]
        for part in range(len(keep))
    ]


def first_sum(keep, got, received):
    sums = []
    for part in range(len(keep)):
        total = first_piece(keep[part], got[part], part, 0)
        for block in received[part]:
            total = total + block.astype(full)
        sums.append(total.astype(low))
    return sums


def second_piece(half, part, step):
    position = ring_order(part)[1][1]
    return lax.dynamic_index_in_dim(half, position ^ step, 1, keepdims=False)


def second_exchange(halves):
    return [
        [swap(second_piece(half, part, step), "dp", step << ring_order(part)[1][2]) for step in (1, 2, 3)]
        for part, half in enumerate(halves)
    ]


def second_sum(halves, received):
    sums = []
    for part, half in enumerate(halves):
        total = second_piece(half, part, 0).astype(full)
        for block in received[part]:
            total = total + block.astype(full)
        sums.append(total.astype(low))
    return jnp.concatenate(sums, axis=2)


def over_group(both):
    me = lax.axis_index("dp") % 4
    table = both[:, :, 1792:].reshape(2, 12, 1024)

    def rows_of(member):
        return jnp.concatenate([lax.dynamic_slice_in_dim(both, member * 12, 12, 1)[:, :, :1792], table], axis=2)

    halves = []
    for core_step in (0, 1):
        blocks = []
        for x_step in (0, 2):
            step = core_step | x_step
            block = rows_of(me ^ step)
            moved = block if step == 0 else swap(block, "dp", step)
            other = lax.ppermute(
                block, ("dp", "seq"), [(i, i ^ (2 * step + 1)) for i in range(lax.axis_size(("dp", "seq")))]
            )
            blocks.append(moved.astype(full) + other.astype(full))
        halves.append((blocks[0] + blocks[1]).astype(low))
    even = lax.axis_index("dp") % 2 == 0
    first, second = jnp.where(even, halves[0], halves[1]), jnp.where(even, halves[1], halves[0])
    total = jnp.stack([first, second], axis=1).reshape(4, 12, 2816)
    return total[:, :, :1792], total[:, :, 1792:].reshape(4, 48, 256)


STEP = 3
LANES = 128 * STEP


def bias_of(row_docs, column_docs, keys_axis, causal):
    shape = (row_docs.shape[0], column_docs.shape[1])
    allowed = row_docs == column_docs
    if causal:
        key = lax.broadcasted_iota(jnp.int32, shape, keys_axis)
        query = lax.broadcasted_iota(jnp.int32, shape, 1 - keys_axis) + (shape[keys_axis] - shape[1 - keys_axis])
        allowed = allowed & (key <= query)
    return jnp.where(allowed, 0.0, masked_out)


def dot_turned(left, right):
    return lax.dot_general(left, right, (((1,), (1,)), ((), ())), preferred_element_type=full)


def both_heads(pair):
    lane = lax.broadcasted_iota(jnp.int32, pair.shape, 1)
    return jnp.concatenate([jnp.where(lane < HD, pair, 0.0), jnp.where(lane < HD, 0.0, pair)], axis=0).astype(low)


def forward_kernel(causal, q_ref, k_ref, v_ref, qd_ref, kd_ref, out_ref, lse_ref, bias):
    @pl.when(pl.program_id(1) == 0)
    def _():
        bias[...] = bias_of(qd_ref[0], kd_ref[0], 1, causal)

    lane = lax.broadcasted_iota(jnp.int32, (ROWS, 128), 1)
    for pair in range(STEP):
        lanes = slice(pair * 128, (pair + 1) * 128)
        queries = both_heads(q_ref[0, :, lanes].astype(full) * scale)
        allowed = bias[...]
        score = dot_turned(queries, k_ref[0, :, lanes]) + jnp.concatenate([allowed, allowed], axis=0)
        maximum = jnp.max(score, axis=1, keepdims=True)
        exponent = jnp.exp(score - maximum)
        total = jnp.sum(exponent, axis=1, keepdims=True)
        prob = (exponent * (1.0 / total)).astype(low)
        out = mm(prob, v_ref[0, :, lanes])
        logs = maximum + jnp.log(total)
        out_ref[0, :, lanes] = jnp.where(lane < HD, out[:ROWS], out[ROWS:]).astype(low)
        lse_ref[0, pair] = jnp.where(lane < 1, logs[:ROWS], logs[ROWS:]).T[:2]


def backward_kernel(causal, q_ref, k_ref, v_ref, kd_ref, qd_ref, do_ref, lse_ref, dq_ref, dk_ref, dv_ref, bias):
    @pl.when(pl.program_id(1) == 0)
    def _():
        bias[...] = bias_of(kd_ref[0], qd_ref[0], 0, causal)

    for pair in range(STEP):
        lanes = slice(pair * 128, (pair + 1) * 128)
        queries = both_heads(q_ref[0, :, lanes].astype(full) * scale)
        grads = both_heads(do_ref[0, :, lanes].astype(full))
        keys, values = k_ref[0, :, lanes], v_ref[0, :, lanes]
        allowed = bias[...]
        logs = jnp.concatenate([lse_ref[0, pair, :1, :], lse_ref[0, pair, 1:, :]], axis=1)
        score = dot_turned(keys, queries) + jnp.concatenate([allowed, allowed], axis=1)
        prob = jnp.exp(score - logs)
        dprob = dot_turned(values, grads)
        inner = jnp.sum(dprob * prob, axis=0, keepdims=True)
        dscore = (prob * (dprob - inner)).astype(low)
        dq = mm(keys.T, dscore) * scale
        dq_ref[0, :, lanes] = jnp.concatenate([dq[:HD, :ROWS], dq[HD:, ROWS:]], axis=0).T.astype(low)
        dk_ref[0, :, lanes] = mm(dscore, queries).astype(low)
        dv_ref[0, :, lanes] = mm(prob.astype(low), grads).astype(low)


def attention_specs(keys, query_block, key_lane, value_lane):
    return [
        pl.BlockSpec((1, ROWS, LANES), lambda p, h: (p, query_block, h)),
        pl.BlockSpec((1, keys, LANES), lambda p, h: (p, 0, key_lane // STEP + h)),
        pl.BlockSpec((1, keys, LANES), lambda p, h: (p, 0, value_lane // STEP + h)),
    ]


def column_row(columns, rows):
    return [
        pl.BlockSpec((1, columns, 1), lambda p, h: (p, 0, 0)),
        pl.BlockSpec((1, 1, rows), lambda p, h: (p, 0, 0)),
    ]


def attend(queries, keys_values, lanes, key_docs, query_docs, causal):
    packs, keys = keys_values.shape[:2]
    query_block = queries.shape[1] // ROWS - 1
    return pl.pallas_call(
        partial(forward_kernel, causal),
        grid=(packs, PAIRS // STEP),
        in_specs=attention_specs(keys, query_block, *lanes) + column_row(ROWS, keys),
        out_specs=[
            pl.BlockSpec((1, ROWS, LANES), lambda p, h: (p, 0, h)),
            pl.BlockSpec((1, STEP, 2, ROWS), lambda p, h: (p, h, 0, 0)),
        ],
        out_shape=[
            jax.ShapeDtypeStruct((packs, ROWS, D), low),
            jax.ShapeDtypeStruct((packs, PAIRS, 2, ROWS), full),
        ],
        scratch_shapes=[pltpu.VMEM((ROWS, keys), full)],
        compiler_params=pltpu.CompilerParams(vmem_limit_bytes=16 * 2**20),
        cost_estimate=pl.CostEstimate(
            flops=4 * packs * HEADS * ROWS * keys * 256,
            bytes_accessed=2 * packs * D * (2 * ROWS + 2 * keys),
            transcendentals=packs * HEADS * ROWS * keys,
        ),
        name="attend",
    )(queries, keys_values, keys_values, query_docs[:, :, None], key_docs[:, None, :])


def attend_back(queries, keys_values, lanes, key_docs, query_docs, causal, grad_out, lse):
    packs, keys = keys_values.shape[:2]
    query_block = queries.shape[1] // ROWS - 1
    own = pl.BlockSpec((1, ROWS, LANES), lambda p, h: (p, 0, h))
    every = pl.BlockSpec((1, keys, LANES), lambda p, h: (p, 0, h))
    return pl.pallas_call(
        partial(backward_kernel, causal),
        grid=(packs, PAIRS // STEP),
        in_specs=attention_specs(keys, query_block, *lanes)
        + column_row(keys, ROWS)
        + [own, pl.BlockSpec((1, STEP, 2, ROWS), lambda p, h: (p, h, 0, 0))],
        out_specs=[own, every, every],
        out_shape=[
            jax.ShapeDtypeStruct((packs, ROWS, D), low),
            jax.ShapeDtypeStruct((packs, keys, D), low),
            jax.ShapeDtypeStruct((packs, keys, D), low),
        ],
        scratch_shapes=[pltpu.VMEM((keys, ROWS), full)],
        compiler_params=pltpu.CompilerParams(vmem_limit_bytes=16 * 2**20),
        cost_estimate=pl.CostEstimate(flops=1, bytes_accessed=1, transcendentals=0),
        name="attend_back",
    )(queries, keys_values, keys_values, key_docs[:, :, None], query_docs[:, None, :], grad_out, lse)


def norm_apply(resid, gains):
    inverse = lax.rsqrt(jnp.mean(resid * resid, axis=-1, keepdims=True) + epsilon)
    return resid * inverse * gains[:, None, :]


def norm_back(resid, gains, grad_norm):
    inverse = lax.rsqrt(jnp.mean(resid * resid, axis=-1, keepdims=True) + epsilon)
    unit = resid * inverse
    grad_gain = jnp.sum(grad_norm * unit, axis=1)
    scaled = grad_norm * gains[:, None, :]
    grad = inverse * (scaled - unit * jnp.mean(scaled * unit, axis=-1, keepdims=True))
    return grad, grad_gain


def gelu_back(pre_act, grad_act):
    _, pull_back = jax.vjp(jax.nn.gelu, pre_act)
    return pull_back(grad_act)[0]


def project(left, weight):
    return jnp.einsum("prd,de->pre", left, weight, preferred_element_type=full)


def project_back(grad_out, weight):
    return jnp.einsum("pre,de->prd", grad_out, weight, preferred_element_type=full)


def weight_grad(left, grad_out):
    return jnp.einsum("prd,pre->de", left, grad_out, preferred_element_type=full)


def adapter_forward(branch, down_gen, up_gen, task_mask):
    branch_low = branch.astype(low)
    pre_act = project(branch_low, down_gen)
    hidden = jnp.where(task_mask, jax.nn.gelu(pre_act), 0.0).astype(low)
    return project(hidden, up_gen), (branch_low, pre_act, hidden)


def adapter_backward(grad_resid, kept, down_gen, up_gen, task_mask):
    branch_low, pre_act, hidden = kept
    grad_adapt = grad_resid.astype(low)
    grad_up = jnp.einsum("prk,prd->pkd", hidden, grad_adapt, preferred_element_type=full)
    grad_hidden = project_back(grad_adapt, up_gen)
    grad_pre = jnp.where(task_mask, gelu_back(pre_act, grad_hidden), 0.0).astype(low)
    grad_down = jnp.einsum("prd,prk->pdk", branch_low, grad_pre, preferred_element_type=full)
    grad_branch = grad_resid + project_back(grad_pre, down_gen)
    return lax.optimization_barrier(
        (
            grad_branch.astype(low),
            jnp.sum(grad_down.astype(low).astype(full), axis=0).astype(low),
            jnp.sum(grad_up.astype(low).astype(full), axis=0)[:WIDE],
        )
    )


def code_table(task_table, place_table, proj_in, proj_out):
    shape = (3, NTASK, TE)
    joined = jnp.concatenate(
        [jnp.broadcast_to(task_table[None], shape), jnp.broadcast_to(place_table[:, None], shape)], axis=-1
    ).reshape(3 * NTASK, 2 * TE)
    hidden = jax.nn.gelu(jnp.dot(joined, proj_in, precision=highest_precision))
    return jnp.dot(hidden, proj_out, precision=highest_precision)


def generate(task_table, place_table, proj_in, proj_out, gen_down, gen_up):
    def body(task, place, first, second, down, up, codes_ref, down_ref, up_ref):
        joined = jnp.concatenate(
            [jnp.concatenate([task[...]] * 3, axis=0)]
            + [jnp.concatenate([jnp.broadcast_to(place[a : a + 1], (NTASK, TE)) for a in range(3)], axis=0)],
            axis=1,
        )
        hidden = jax.nn.gelu(jnp.dot(joined, first[...], precision=highest_precision))
        codes = jnp.dot(hidden, second[...], precision=highest_precision).astype(low)
        codes_ref[...] = codes
        down_ref[...] = mm(codes, down[...]).astype(low)
        up_ref[...] = mm(codes, up[...]).astype(low)

    count = 3 * NTASK
    return pl.pallas_call(
        body,
        out_shape=[jax.ShapeDtypeStruct((count, width), low) for width in (TE, 288, 288)],
        name="generate",
    )(task_table, place_table, proj_in, proj_out, gen_down, gen_up)


def up_to_block(rows):
    lead = rows.shape[:-2]
    tiles = jnp.moveaxis(rows.reshape(*lead, 8, 9, 128), -2, -3).reshape(*lead, 72, 128)
    tiles = jnp.pad(tiles, [(0, 0)] * len(lead) + [(0, 24), (0, 0)]).reshape(*lead, 2, 48, 128)
    return jnp.moveaxis(tiles, -3, -2).reshape(*lead, 48, 256)


def up_from_block(block):
    lead = block.shape[:-2]
    tiles = jnp.moveaxis(block.reshape(*lead, 48, 2, 128), -2, -3).reshape(*lead, 96, 128)[..., :72, :]
    return jnp.moveaxis(tiles.reshape(*lead, 9, 8, 128), -3, -2).reshape(*lead, 8, 1152)


def over_dp(value):
    for shift in (0, 2, 4):
        first = value + swap(value, "dp", 1 << shift)
        second = swap(value, "dp", 2 << shift) + swap(value, "dp", 3 << shift)
        value = first + second
    return value


def both_halves(part):
    return part.astype(full) + swap(part, "seq", 1).astype(full)


def shards(
    inputs,
    memory,
    cotangent,
    seg_ids,
    mem_seg,
    tasks,
    self_qkv,
    self_out,
    cross_query,
    cross_kv,
    cross_out,
    ff_in,
    ff_out,
    gen_down,
    gen_up,
    gen_gain,
    task_table,
    place_table,
    proj_in,
    proj_out,
):
    seq_index = lax.axis_index("seq")
    core = lax.axis_index("dp") % 2
    packs, row_count = inputs.shape[:2]
    mem_count = memory.shape[1]

    _, hyper_pull = jax.vjp(code_table, task_table, place_table, proj_in, proj_out)
    codes_low, own_down, own_up = generate(task_table, place_table, proj_in, proj_out, gen_down, gen_up)
    own_down = own_down.reshape(3, NTASK, 12, R)
    own_down = own_down.transpose(2, 0, 3, 1).reshape(12, 3, WIDE)
    spare = jnp.pad(gen_gain.T[:, None, :], ((0, 0), (0, 2), (0, 0)))
    own_down = jnp.concatenate([own_down, spare], axis=2).reshape(12, 3 * PLACE)
    up_pieces = jnp.pad(own_up.reshape(3, 12, 192), ((0, 1), (0, 0), (0, 64)))
    early = jnp.concatenate([self_qkv, own_down[:, :PLACE]], axis=1).reshape(12, 4, EARLY)
    late = [self_out, cross_query, cross_out, cross_kv, own_down[:, PLACE:], jnp.zeros((12, 256), low), ff_in]
    late = jnp.concatenate(late, axis=1).reshape(12, 4, QUARTER)
    exchanged = group_exchange(
        jnp.concatenate([jnp.concatenate([early, late], axis=2).transpose(1, 0, 2), up_pieces], axis=2)
    )
    early = exchanged[:, :, :EARLY].reshape(48, EARLY)
    late = exchanged[:, :, EARLY:2560].reshape(48, QUARTER)
    up_rows = exchanged[:, :, 2560:2752].reshape(4, NTASK, 288).transpose(1, 0, 2).reshape(NTASK, 1152)
    block = jnp.concatenate([late, ff_out, up_to_block(up_rows)], axis=1)

    gathered = lax.all_gather(block, "dp", axis=0, tiled=False)
    ids = jnp.concatenate([seg_ids, mem_seg], axis=1)
    early, other_ids, other_memory, earlier = lax.optimization_barrier(
        (
            early_gather(early),
            swap(ids, "seq", 1),
            swap(memory, "seq", 1),
            lax.ppermute(inputs, "seq", [(0, 1)]),
        )
    )
    mem_rows = jnp.concatenate([memory, other_memory], axis=1)
    mem_docs = jnp.concatenate([mem_seg, other_ids[:, row_count:]], axis=1)
    earlier_docs = jnp.where(seq_index > 0, other_ids[:, :row_count], -1)
    key_docs = jnp.concatenate([earlier_docs, seg_ids], axis=1)
    query_docs = seg_ids

    early = unpack_early(early, swap(early, "dp", 1))
    full_self_qkv, down_zero = [piece.reshape(D, piece.shape[2]) for piece in early]
    pieces = unpack(gathered.reshape(16, 4, 48, 2944))
    full_self_out, full_query, full_cross_out, full_mem_kv, full_down, full_ff_in = [
        piece.reshape(D, piece.shape[2]) for piece in pieces[:6]
    ]
    full_ff_out = pieces[6].reshape(FF, D)
    full_up = jnp.pad(pieces[7].astype(low), ((0, 0), (0, PLACE - WIDE), (0, 0)))
    full_gain = down_zero[:, WIDE:]
    down_of = [down_zero, full_down[:, :PLACE], full_down[:, PLACE:]]
    up_of = [full_up[a] for a in range(3)]

    gain_table = 1.0 + jnp.einsum("xt,ct->xc", codes_low, full_gain, preferred_element_type=full)
    onehot = (tasks[:, None] == jnp.arange(NTASK, dtype=jnp.int32)[None, :]).astype(full)
    gain_all = jnp.einsum(
        "pt,atc->pac", onehot, gain_table.reshape(3, NTASK, D), precision=highest_precision
    )
    column = jnp.arange(PLACE, dtype=jnp.int32)
    task_mask = ((tasks[:, None] == (column % NTASK)[None, :]) & (column < WIDE)[None, :])[:, None, :]

    both_rows = jnp.concatenate([earlier, inputs], axis=1).astype(full)
    resid_zero = both_rows[:, row_count:]
    normed_one = norm_apply(both_rows, gain_all[:, 0]).astype(low)
    self_proj = project(normed_one, full_self_qkv).astype(low)
    mem_kv = project(mem_rows, full_mem_kv).astype(low)
    attended_one, total_one = attend(self_proj, self_proj, (6, 12), key_docs, query_docs, True)
    branch_one = project(attended_one, full_self_out)
    adapt_one, kept_one = adapter_forward(branch_one, down_of[0], up_of[0], task_mask)
    resid_one = resid_zero + branch_one + adapt_one
    normed_two = norm_apply(resid_one, gain_all[:, 1]).astype(low)
    cross_queries = project(normed_two, full_query).astype(low)
    attended_two, total_two = attend(cross_queries, mem_kv, (0, 6), mem_docs, query_docs, False)
    branch_two = project(attended_two, full_cross_out)
    adapt_two, kept_two = adapter_forward(branch_two, down_of[1], up_of[1], task_mask)
    resid_two = resid_one + branch_two + adapt_two
    normed_three = norm_apply(resid_two, gain_all[:, 2]).astype(low)
    ff_pre = project(normed_three, full_ff_in)
    ff_hidden = jax.nn.gelu(ff_pre).astype(low)
    branch_three = project(ff_hidden, full_ff_out)
    adapt_three, kept_three = adapter_forward(branch_three, down_of[2], up_of[2], task_mask)
    mixed = (resid_two + branch_three + adapt_three).astype(low)

    grad_three = cotangent.astype(full)
    branch_grad, down_three, up_three = adapter_backward(grad_three, kept_three, down_of[2], up_of[2], task_mask)
    grad_ff_out = weight_grad(ff_hidden, branch_grad).astype(low)
    hidden_grad = project_back(branch_grad, full_ff_out)
    pre_grad = gelu_back(ff_pre, hidden_grad).astype(low)
    grad_ff_in = weight_grad(normed_three, pre_grad).astype(low)
    resid_grad, gain_three = norm_back(resid_two, gain_all[:, 2], project_back(pre_grad, full_ff_in))
    grad_two = grad_three + resid_grad
    ff_blocks, grad_two = lax.optimization_barrier((pack_ff(grad_ff_in, grad_ff_out), grad_two))
    part_ff = lax.psum_scatter(ff_blocks, "dp", scatter_dimension=0, tiled=False)[:96]

    branch_grad, down_two, up_two = adapter_backward(grad_two, kept_two, down_of[1], up_of[1], task_mask)
    grad_two_low = branch_grad
    out_grad = project_back(branch_grad, full_cross_out).astype(low)
    query_two, key_two, value_two = attend_back(
        cross_queries, mem_kv, (0, 6), mem_docs, query_docs, False, out_grad, total_two
    )
    rows_grad = project_back(key_two, full_mem_kv[:, :D]) + project_back(value_two, full_mem_kv[:, D:])
    grad_memory = rows_grad[:, :mem_count] + swap(rows_grad[:, mem_count:].astype(low), "seq", 1).astype(full)
    resid_grad, gain_two = norm_back(resid_one, gain_all[:, 1], project_back(query_two, full_query))
    grad_one = grad_two + resid_grad

    branch_grad, down_one, up_one = adapter_backward(grad_one, kept_one, down_of[0], up_of[0], task_mask)
    grad_one_low = branch_grad
    gain_sum = jnp.einsum("pt,pac->atc", onehot, jnp.stack([gain_two, gain_three], 1), precision=highest_precision)
    gain_sum = gain_sum.reshape(2 * NTASK, D)
    codes_full = codes_low.astype(full)
    spare_codes = jnp.pad(codes_full[NTASK:], ((0, 0), (WIDE, 0)))
    grad_gain = jnp.einsum("xc,xt->ct", gain_sum, spare_codes, precision=highest_precision).astype(low)
    out_grad = project_back(branch_grad, full_self_out).astype(low)
    query_grad, key_grad, value_grad = attend_back(
        self_proj, self_proj, (6, 12), key_docs, query_docs, True, out_grad, total_one
    )
    norm_grad = project_back(key_grad, full_self_qkv[:, D : 2 * D]) + project_back(
        value_grad, full_self_qkv[:, 2 * D :]
    )
    returned = lax.ppermute(norm_grad[:, :row_count].astype(low), "seq", [(1, 0)])
    keep, send = pack_gradients(
        core,
        [
            (attended_one, 0, ROWS),
            (normed_two, 0, ROWS),
            (attended_two, 0, ROWS),
            (mem_rows, 0, 2 * mem_count),
            (normed_one, 1, ROWS),
            (normed_one, 0, 2 * ROWS),
        ],
        [
            (0, grad_one_low, 0),
            (1, query_two, 0),
            (2, grad_two_low, 0),
            (3, key_two, 0),
            (3, value_two, 0),
            (4, query_grad, 0),
            (5, key_grad, 0),
            (5, value_grad, 0),
        ],
        (down_one, down_two, down_three),
        grad_gain,
        (up_one, up_two, up_three),
        (1024, 1024),
    )
    got = over_cores(send)
    received = first_exchange(keep, got)
    norm_grad = norm_grad[:, row_count:] + project_back(query_grad, full_self_qkv[:, :D]) + returned.astype(full)
    resid_grad, gain_one = norm_back(resid_zero, gain_all[:, 0], norm_grad)
    grad_input = grad_one + resid_grad
    gain_first = jnp.einsum("pt,pc->tc", onehot, gain_one, precision=highest_precision)
    gain_codes = jnp.einsum("xc,ct->xt", gain_sum, full_gain.astype(full), precision=highest_precision)
    gain_part = jnp.concatenate(
        [gain_first.reshape(3 * NTASK, 256), jnp.pad(gain_codes, ((NTASK, 0), (0, 0)))], axis=1
    )
    gain_part = gain_part + swap(gain_part, "seq", 1)
    halves = first_sum(keep, got, received)
    both = second_sum(halves, second_exchange(halves))
    pieces, up_blocks = over_group(both)
    rest = pieces.transpose(1, 0, 2).reshape(12, 7168).astype(full)
    up_rows = up_from_block(up_blocks[:3]).reshape(3 * NTASK, 1152)
    up_table = lax.dynamic_slice_in_dim(up_rows, (lax.axis_index("dp") % 4) * 288, 288, 1).astype(full)
    sum_self_out = rest[:, :768]
    sum_query = rest[:, 768:1536]
    sum_cross_out = rest[:, 1536:2304]
    sum_mem_kv = rest[:, 2304:3840]
    down_table = rest[:, 3840:4608].reshape(12, 3, PLACE)[:, :, :WIDE].reshape(12, 3, R, NTASK)
    down_table = down_table.transpose(1, 3, 0, 2).reshape(3 * NTASK, 288)
    sum_qkv = rest[:, 4608:6912]
    sum_down = jnp.einsum("xt,xc->tc", codes_full, down_table, precision=highest_precision)
    sum_up = jnp.einsum("xt,xc->tc", codes_full, up_table, precision=highest_precision)

    grad_codes = jnp.einsum("xc,tc->xt", down_table, gen_down.astype(full), precision=highest_precision) + jnp.einsum(
        "xc,tc->xt", up_table, gen_up.astype(full), precision=highest_precision
    )
    joint = gain_part + jnp.pad(grad_codes, ((0, 0), (256, 0)))
    joint, part_ff = lax.optimization_barrier((over_dp(joint), part_ff))
    part_ff = both_halves(part_ff)
    sum_ff_in = from_quarters(part_ff[:48].astype(low)).astype(full)
    sum_ff_out = part_ff[48:]
    gain_first = joint[:, :256].reshape(NTASK, D)
    first_codes = jnp.einsum("xc,ct->xt", gain_first, full_gain.astype(full), precision=highest_precision)
    grad_codes = joint[:, 256:] + jnp.pad(first_codes, ((0, 2 * NTASK), (0, 0)))
    table_sum, place_sum, proj_in_sum, proj_out_sum = hyper_pull(grad_codes)
    own_gains = lax.dynamic_slice_in_dim(gain_first, lax.axis_index("dp") * 12, 12, 1)
    sum_gain = jnp.einsum("xt,xc->tc", codes_full[:NTASK], own_gains, precision=highest_precision)
    sum_gain = sum_gain + rest[:, 3840 + WIDE : 3840 + PLACE].T
    return (
        mixed,
        grad_input,
        grad_memory,
        sum_qkv,
        sum_self_out,
        sum_query,
        sum_mem_kv,
        sum_cross_out,
        sum_ff_in,
        sum_ff_out,
        sum_down,
        sum_up,
        sum_gain,
        table_sum,
        place_sum,
        proj_in_sum,
        proj_out_sum,
    )


def solution(mesh):
    in_specs = (
        P("dp", "seq", None),
        P("dp", "seq", None),
        P("dp", "seq", None),
        P("dp", "seq"),
        P("dp", "seq"),
        P("dp"),
        P("dp", None),
        P("dp", None),
        P("dp", None),
        P("dp", None),
        P("dp", None),
        P("dp", None),
        P("dp", None),
        P(None, "dp"),
        P(None, "dp"),
        P(None, "dp"),
        P(),
        P(),
        P(),
        P(),
    )
    out_specs = (
        P("dp", "seq", None),
        P("dp", "seq", None),
        P("dp", "seq", None),
        P("dp", None),
        P("dp", None),
        P("dp", None),
        P("dp", None),
        P("dp", None),
        P("dp", None),
        P("dp", None),
        P(None, "dp"),
        P(None, "dp"),
        P(None, "dp"),
        P(),
        P(),
        P(),
        P(),
    )
    return jax.shard_map(shards, mesh=mesh, in_specs=in_specs, out_specs=out_specs, check_vma=False)
```
